32 devices in a mesh: grp: 2 (over x), col: 16 (over z, y, core).
Axes of the slice: x: 2, y: 2, z: 4, core: 2. Of those that a mesh axis runs over, the one named last changes fastest.
Arguments:
- lam_in: float32 [320, 4, 32, 128], P('grp', None, 'col'), parts along dimension 0, may hold values from -0.5 to 1.5
- conc: float32 [320, 4, 32, 128], P('grp', None, 'col'), parts along dimension 0, may hold values from 0.3 to 3
- jac_diag: bfloat16 [20, 16, 16, 4, 32, 128], P('grp', None, None, None, 'col'), parts along dimension 0, may hold values from -0.59765625 to 0.59765625
- jac_off: bfloat16 [8, 16, 16, 4, 32, 128], P('grp', None, None, None, 'col'), parts along dimension 0, may hold values from -0.59765625 to 0.59765625
- block_rows: int32 [8, 4, 32, 128], P('grp', None, 'col'), parts along dimension 0, may hold values from 0 to 9
- block_cols: int32 [8, 4, 32, 128], P('grp', None, 'col'), parts along dimension 0, may hold values from 0 to 9
- active: int32 [8, 32, 128], P('grp', 'col'), parts along dimension 0, may hold values from 0 to 4
- courant: float32 [2, 8, 32, 128], P(None, 'grp', 'col'), parts along dimension 1, may hold values from 0.05 to 0.45
- kz: float32 [6, 32, 128], P('grp', 'col'), parts along dimension 0, may hold values from 0.1 to 3
- airmass: float32 [8, 32, 128], P('grp', 'col'), parts along dimension 0, may hold values from 0.5 to 6, as said below
- target: float32 [320], P('grp'), parts along dimension 0, may hold values from 0.5 to 2
- emis_map: float32 [64, 160], replicated, may hold values from -0.5 to 0.5
Outputs:
- lam_out: float32 [320, 4, 32, 128], P('grp', None, 'col'), parts along dimension 0
- grad_emis: float32 [128, 32, 128], P('grp', 'col'), parts along dimension 0
The draws below stay inside these ranges and needn't reach their ends.
There are 2 independent parts, one for each index of `grp`. The reference program is written for one: setup_inputs(seed, part) draws one part's arguments, and reference() takes and returns one part's arrays. A program takes and returns all parts, laid end to end along the dimension named above; an argument that names none is the same for every part. Nothing has to cross between parts.
Inputs may be any that keep to these rules, and one draw needn't show every extreme that they name: airmass is positive. Slots p >= active[cell] are ignored.
All inputs are finite; a program needn't handle non-finite values.
Results may differ from the reference program's by a relative error of at most 0.0003.
Values sent between devices are 32-bit elements; how exact they have to be, the bound alone decides.
A program may use at most 64 MiB of HBM per device.

```python
import math
import jax
import jax.numpy as jnp
from jax import lax

S = 160
BS = 16
NB = 10
P_SIZE = 4
E = 64
LEV = 4
ADV = 2
NY = 128
NX = 32


def draw_airmass(key, part):
    key = jax.random.fold_in(key, 7)
    across = jnp.arange(NX, dtype=jnp.float32) / max(NX - 1, 1)
    trend = 1.0 + 2.0 * across[None, :, None]
    base = jnp.exp(jax.random.uniform(key, (LEV, NX, NY), jnp.float32, jnp.log(0.5), jnp.log(2.0)))
    return trend * base


def place_ends(values, key, low, top_value):
    longest = values.shape.index(max(values.shape))
    spots = []
    for shift in (0, 1):
        where = [jax.random.randint(jax.random.fold_in(key, axis), (), 0, length) for axis, length in enumerate(values.shape)]
        where[longest] = (where[longest] + shift) % values.shape[longest]
        spots.append(tuple(where))
    return values.at[spots[0]].set(low).at[spots[1]].set(top_value)


def block_levels(rng, shape, shards, smallest, high):
    factor_of, own = 1.0, jax.random.fold_in(rng, 6)
    for axis_at, parts in shards:
        heights = jnp.exp(jax.random.uniform(jax.random.fold_in(own, axis_at), (parts,), jnp.float32, smallest / len(shards), high / len(shards)))
        factor_of = factor_of * jnp.repeat(heights, shape[axis_at] // parts).reshape([-1 if axis == axis_at else 1 for axis in range(len(shape))])
    return factor_of


def bell_draw(rng, shape, width, bound, pieces=(), kind=jnp.bfloat16):
    factor_of = block_levels(rng, shape, pieces, -0.22, 0.18) if pieces else 1.0
    values = jax.random.normal(rng, shape, jnp.float32) * width * factor_of
    return jnp.minimum(jnp.maximum(values, -bound), bound).astype(kind)


def setup_inputs(seed: int = 0, part: int = 0) -> dict:
    key_list = jax.random.split(jax.random.key(seed), 13)
    part_splits = jax.random.split(jax.random.fold_in(key_list[12], part), 13)
    lam_in = jnp.clip(-0.5 + 2.0 * jax.random.uniform(part_splits[0], (S, LEV, NX, NY), jnp.float32) ** block_levels(part_splits[0], (S, LEV, NX, NY), ((2, 16),), -0.2, 0.2), -0.5, 1.5)
    conc = jnp.clip(jnp.exp(math.log(3.0) - 2.3025851 * jax.random.uniform(part_splits[1], (S, LEV, NX, NY), jnp.float32) ** block_levels(part_splits[1], (S, LEV, NX, NY), ((2, 16),), -0.2, 0.2)), 0.3, 3.0)
    jac_diag = bell_draw(part_splits[2], (NB, BS, BS, LEV, NX, NY), 0.12, 0.59765625, ((4, 16),))
    jac_off = bell_draw(part_splits[3], (P_SIZE, BS, BS, LEV, NX, NY), 0.12, 0.59765625, ((4, 16),))
    block_rows = place_ends(jax.random.randint(part_splits[4], (P_SIZE, LEV, NX, NY), 0, NB), jax.random.fold_in(part_splits[4], 1), 0, NB - 1).astype(jnp.int32)
    block_cols = place_ends(jax.random.randint(part_splits[5], (P_SIZE, LEV, NX, NY), 0, NB), jax.random.fold_in(part_splits[5], 1), 0, NB - 1).astype(jnp.int32)
    active = place_ends(jax.random.randint(part_splits[6], (LEV, NX, NY), 0, P_SIZE + 1), jax.random.fold_in(part_splits[6], 1), 0, P_SIZE).astype(jnp.int32)
    courant = jnp.clip(0.05 + 0.39999999 * jax.random.uniform(part_splits[7], (2, LEV, NX, NY), jnp.float32) ** block_levels(part_splits[7], (2, LEV, NX, NY), ((2, 16),), -0.2, 0.2), 0.05, 0.45)
    kz = jnp.clip(jnp.exp(math.log(3.0) - 3.4011974 * jax.random.uniform(part_splits[8], (LEV - 1, NX, NY), jnp.float32) ** block_levels(part_splits[8], (LEV - 1, NX, NY), ((1, 16),), -0.2, 0.2)), 0.1, 3.0)
    airmass = draw_airmass(jax.random.fold_in(jax.random.fold_in(key_list[12], part), 71), part)
    target = jnp.clip(jnp.exp(jax.random.uniform(part_splits[10], (S,), jnp.float32, math.log(0.5), math.log(2.0))), 0.5, 2.0)
    emis_map = bell_draw(key_list[11], (E, S), S ** -0.5, 0.5, (), jnp.float32)
    return dict(lam_in=lam_in, conc=conc, jac_diag=jac_diag, jac_off=jac_off, block_rows=block_rows, block_cols=block_cols, active=active, courant=courant, kz=kz, airmass=airmass, target=target, emis_map=emis_map)


def chem_adjoint(lam, jac_diag, jac_off, block_rows, block_cols, active):
    nblocks = jac_diag.shape[0]
    bsize = jac_diag.shape[1]
    lamb = lam.reshape((nblocks, bsize) + lam.shape[1:])
    result = lamb + jnp.einsum('bij...,bi...->bj...', jac_diag.astype(jnp.float32), lamb, precision=lax.Precision.HIGHEST)
    blocks = jnp.arange(nblocks, dtype=jnp.int32)
    for slot in range(jac_off.shape[0]):
        pick = (block_rows[slot][None] == blocks[:, None, None, None]).astype(jnp.float32)
        chosen = jnp.sum(pick[:, None] * lamb, axis=0)
        live = (active > slot).astype(jnp.float32)
        contrib = jnp.einsum('ij...,i...->j...', jac_off[slot].astype(jnp.float32), chosen, precision=lax.Precision.HIGHEST) * live[None]
        place = (block_cols[slot][None] == blocks[:, None, None, None]).astype(jnp.float32)
        result = result + place[:, None] * contrib[None]
    return result.reshape(lam.shape)


def solve_levels(kz, rhs):
    levels = rhs.shape[1]
    diag = []
    for lev in range(levels):
        value = jnp.ones_like(rhs[0, 0])
        if lev > 0:
            value = value + kz[lev - 1]
        if lev < levels - 1:
            value = value + kz[lev]
        diag.append(value)
    cprime = []
    dprime = []
    for lev in range(levels):
        denom = diag[lev]
        numer = rhs[:, lev]
        if lev > 0:
            denom = denom + kz[lev - 1] * cprime[lev - 1]
            numer = numer + kz[lev - 1] * dprime[lev - 1]
        denom = denom[None]
        cval = -kz[lev][None] / denom if lev < levels - 1 else None
        cprime.append(cval[0] if cval is not None else None)
        dprime.append(numer / denom)
    solved = [None] * levels
    solved[levels - 1] = dprime[levels - 1]
    for lev in range(levels - 2, -1, -1):
        solved[lev] = dprime[lev] - cprime[lev][None] * solved[lev + 1]
    return jnp.stack(solved, axis=1)


def advect_back(lam, right_out, left_out):
    padded = jnp.pad(lam, ((0, 0), (0, 0), (1, 1), (0, 0)))
    return padded[:, :, 1:-1] * (1.0 - right_out - left_out) + left_out * padded[:, :, :-2] + right_out * padded[:, :, 2:]


def reference(lam_in, conc, jac_diag, jac_off, block_rows, block_cols, active, courant, kz, airmass, target, emis_map):
    lam = chem_adjoint(lam_in, jac_diag, jac_off, block_rows, block_cols, active)
    mass = jnp.sum(conc * airmass[None], axis=(1, 2, 3))
    quad = jnp.sum(conc * lam, axis=(1, 2, 3))
    cells = LEV * NX * NY
    scale = target * cells / mass
    lam = lam * scale[:, None, None, None] - airmass[None] * (scale * quad / mass)[:, None, None, None]
    lam = solve_levels(kz, lam)
    for step in range(ADV):
        lam = advect_back(lam, courant[0][None], courant[1][None])
    grad_emis = jnp.einsum('es,sxy->exy', emis_map, lam[:, 0], precision=lax.Precision.HIGHEST)
    return lam, grad_emis
```

```python
import functools

import jax
import jax.numpy as jnp
from jax import lax
from jax.experimental import pallas as pl
from jax.experimental.pallas import tpu as pltpu
from jax.sharding import PartitionSpec as P

ADV = 2
ROWS = 8
LANES = 128
F32 = jnp.float32


def inverse_levels(kz):
    levels = len(kz) + 1
    diag = []
    for lev in range(levels):
        value = jnp.ones_like(kz[0])
        if lev > 0:
            value = value + kz[lev - 1]
        if lev < levels - 1:
            value = value + kz[lev]
        diag.append(value)
    cprime, recip = [], []
    for lev in range(levels):
        denom = diag[lev]
        if lev > 0:
            denom = denom + kz[lev - 1] * cprime[lev - 1]
        recip.append(1.0 / denom)
        cprime.append(-kz[lev] * recip[lev] if lev < levels - 1 else None)
    result = [[None] * levels for _ in range(levels)]
    for unit in range(levels):
        dprime = []
        for lev in range(levels):
            if lev < unit:
                dprime.append(jnp.zeros_like(kz[0]))
            elif lev == unit:
                dprime.append(recip[lev])
            else:
                dprime.append(kz[lev - 1] * dprime[lev - 1] * recip[lev])
        solved = dprime[levels - 1]
        result[levels - 1][unit] = solved
        for lev in range(levels - 2, -1, -1):
            solved = dprime[lev] - cprime[lev] * solved
            result[lev][unit] = solved
    return result


def up(x):
    return pltpu.roll(x, ROWS - 1, x.ndim - 2)


def down(x):
    return pltpu.roll(x, 1, x.ndim - 2)


def kernel(
    nblocks, bsize, slots, levels, cells, n,
    lam_h, conc_h, jd_h, jo_h, rows_h, cols_h, act_h, cour_h, kz_h, air_h, target_h, emis_h,
    out_h, grad_h,
    lam, conc, jd, jo, rows, cols, act, cour, kz, air, target, emis,
    l0, left, right, out, grad, contrib, solve, small, small_l, small_r,
    part, stat, stats, scol, gcol,
    in_sem, jo_sem, jd_sem, out_sem, send_r, send_l, recv_l, recv_r, ssem, stat_send, stat_recv,
):
    me = lax.axis_index("col")
    species = nblocks * bsize
    bl = bsize * ROWS
    step = bsize * bl

    def peer(k):
        return lax.rem(me + k, n)

    barrier = pltpu.get_barrier_semaphore()

    @pl.loop(1, n)
    def _(k):
        pl.semaphore_signal(
            barrier, inc=1, device_id={"col": peer(k)}, device_id_type=pl.DeviceIdType.MESH
        )

    plain = [
        pltpu.make_async_copy(src, dst, in_sem.at[k])
        for k, (src, dst) in enumerate(
            [
                (lam_h, lam), (rows_h, rows), (cols_h, cols), (act_h, act), (kz_h, kz),
                (cour_h, cour), (air_h, air), (target_h, target), (emis_h, emis), (conc_h, conc),
            ]
        )
    ]

    def jo_copy(p):
        at = pl.ds(pl.multiple_of(p * step, step), step)
        return pltpu.make_async_copy(jo_h.at[at], jo.at[at], jo_sem.at[p])

    def jd_copy(c):
        at = pl.ds(pl.multiple_of(c * step, step), step)
        return pltpu.make_async_copy(jd_h.at[at], jd.at[at], jd_sem.at[c])

    for copy in plain[:8]:
        copy.start()
    for p in range(slots):
        jo_copy(p).start()
    for c in range(nblocks):
        jd_copy(c).start()
        if c == 0:
            plain[9].start()
    plain[8].start()

    @pl.when(me == 0)
    def _():
        left[...] = jnp.zeros_like(left)
        small_l[...] = jnp.zeros_like(small_l)

    @pl.when(me == n - 1)
    def _():
        right[...] = jnp.zeros_like(right)
        small_r[...] = jnp.zeros_like(small_r)

    for copy in plain[1:8]:
        copy.wait()

    kzs = [kz[lev] for lev in range(levels - 1)]
    inverse = inverse_levels(kzs)
    for shift in range(levels):
        for lev in range(levels):
            solve[shift, 2 * lev : 2 * lev + 2, :] = inverse[lev][(lev - shift) % levels]

    def solve_levels(x):
        total = x * solve[0]
        for shift in range(1, levels):
            total = total + pltpu.roll(x, 2 * shift, x.ndim - 2) * solve[shift]
        return total

    small[0:8, :] = cour[0:8, :]
    small[8:16, :] = cour[8:16, :]
    small[16:24, :] = solve_levels(air[...])

    plain[0].wait()

    @pl.loop(0, slots)
    def _(p):
        live = act[...] > p
        want = jnp.where(live, rows[pl.ds(pl.multiple_of(p * ROWS, ROWS), ROWS), :], -1)
        chosen = jnp.zeros((bsize, ROWS, LANES), F32)
        for b in range(nblocks):
            block = lam[b * bl : (b + 1) * bl, :].reshape(bsize, ROWS, LANES)
            chosen = jnp.where((want == b)[None], block, chosen)
        jo_copy(p).wait()
        acc = jnp.zeros((bsize, ROWS, LANES), F32)
        for i in range(bsize):
            at = pl.ds(pl.multiple_of(p * step + i * bl, bl), bl)
            acc = acc + jo[at, :].astype(F32).reshape(bsize, ROWS, LANES) * chosen[i][None]
        contrib[p] = acc

    pl.semaphore_wait(barrier, n - 1)

    def to_right(src, dst, ssem_, rsem):
        return pltpu.make_async_remote_copy(
            src_ref=src, dst_ref=dst, send_sem=ssem_, recv_sem=rsem,
            device_id={"col": jnp.minimum(me + 1, n - 1)}, device_id_type=pl.DeviceIdType.MESH,
        )

    def to_left(src, dst, ssem_, rsem):
        return pltpu.make_async_remote_copy(
            src_ref=src, dst_ref=dst, send_sem=ssem_, recv_sem=rsem,
            device_id={"col": jnp.maximum(me - 1, 0)}, device_id_type=pl.DeviceIdType.MESH,
        )

    def block_at(c):
        return pl.ds(pl.multiple_of(c * bl, bl), bl)

    def block_right(c):
        return to_right(l0.at[block_at(c)], left.at[block_at(c)], send_r.at[c], recv_l.at[c])

    def block_left(c):
        return to_left(l0.at[block_at(c)], right.at[block_at(c)], send_l.at[c], recv_r.at[c])

    small_right = to_right(small, small_l, ssem.at[0], ssem.at[1])
    small_left = to_left(small, small_r, ssem.at[2], ssem.at[3])

    @pl.when(me < n - 1)
    def _():
        small_right.start()

    @pl.when(me > 0)
    def _():
        small_left.start()

    plain[9].wait()

    @pl.loop(0, nblocks)
    def _(c):
        block = lam[block_at(c), :].reshape(bsize, ROWS, LANES)
        jd_copy(c).wait()
        acc = block
        for i in range(bsize):
            at = pl.ds(pl.multiple_of(c * step + i * bl, bl), bl)
            acc = acc + jd[at, :].astype(F32).reshape(bsize, ROWS, LANES) * block[i][None]
        for p in range(slots):
            place = cols[p * ROWS : (p + 1) * ROWS, :] == c
            acc = acc + jnp.where(place[None], contrib[p], 0.0)
        l0[block_at(c), :] = solve_levels(acc).reshape(bl, LANES)

        @pl.when(me < n - 1)
        def _():
            block_right(c).start()

        @pl.when(me > 0)
        def _():
            block_left(c).start()

        amount = conc[block_at(c), :].reshape(bsize, ROWS, LANES)
        at = pl.ds(pl.multiple_of(c * bsize, bsize), bsize)
        part[0, at, :] = jnp.sum(amount * air[...][None], axis=1)
        part[1, at, :] = jnp.sum(amount * acc, axis=1)

    tail = species - LANES
    for which in range(2):
        for half, first in enumerate((0, tail)):
            square = part[which, first : first + LANES, :]
            stat[2 * which + half : 2 * which + half + 1, :] = jnp.sum(
                square.T, axis=0, keepdims=True
            )

    def stat_copy(k):
        return pltpu.make_async_remote_copy(
            src_ref=stat, dst_ref=stats.at[me], send_sem=stat_send.at[k], recv_sem=stat_recv.at[me],
            device_id={"col": peer(k)}, device_id_type=pl.DeviceIdType.MESH,
        )

    def stat_from(k):
        source = lax.rem(me + n - k, n)
        return source, pltpu.make_async_remote_copy(
            src_ref=stat, dst_ref=stats.at[source], send_sem=stat_send.at[k],
            recv_sem=stat_recv.at[source],
            device_id={"col": peer(k)}, device_id_type=pl.DeviceIdType.MESH,
        )

    @pl.loop(1, n)
    def _(k):
        stat_copy(k).start()

    @pl.when(me > 0)
    def _():
        to_right(small, small_l, ssem.at[0], ssem.at[1]).wait_recv()

    @pl.when(me < n - 1)
    def _():
        to_left(small, small_r, ssem.at[2], ssem.at[3]).wait_recv()

    even = lax.rem(lax.broadcasted_iota(jnp.int32, (ROWS, LANES), 0), 2) == 0

    def swap(x):
        return jnp.where(even, up(x), down(x))

    a, b = small[0:8, :], small[8:16, :]
    c = 1.0 - a - b
    al, bl_ = small_l[0:8, :], small_l[8:16, :]
    cl = 1.0 - al - bl_
    ar, br = small_r[0:8, :], small_r[8:16, :]
    cr = 1.0 - ar - br
    own_same = c * c + jnp.where(even, b * swap(al) + a * swap(b), b * swap(a) + a * swap(br))
    own_swap = jnp.where(even, a, b) * (c + swap(c))
    left_same = b * jnp.where(even, swap(bl_), swap(b))
    left_up = jnp.where(even, b * (c + swap(cl)), 0.0)
    right_same = a * jnp.where(even, swap(a), swap(ar))
    right_down = jnp.where(even, 0.0, a * (c + swap(cr)))

    def advect(mid, lt, rt):
        return (
            own_same * mid
            + own_swap * jnp.where(even, up(mid), down(mid))
            + left_same * lt
            + left_up * up(lt)
            + right_same * rt
            + right_down * down(rt)
        )

    air_out = advect(small[16:24, :], small_l[16:24, :], small_r[16:24, :])

    def add_stat(k, total):
        source, copy = stat_from(k)
        copy.wait_recv()
        return total + stats[source]

    total = lax.fori_loop(1, n, add_stat, stat[...])
    for half, first in enumerate((0, tail)):
        mass = total[half : half + 1, :]
        quad = total[2 + half : 3 + half, :]
        scale = target[:, first : first + LANES] * float(cells) / mass
        gain = scale * quad / mass
        scol[first : first + LANES, :] = jnp.broadcast_to(scale, (LANES, LANES)).T
        gcol[first : first + LANES, :] = jnp.broadcast_to(gain, (LANES, LANES)).T

    def out_copy(c):
        return pltpu.make_async_copy(out.at[block_at(c)], out_h.at[block_at(c)], out_sem.at[c])

    @pl.loop(0, nblocks)
    def _(c):
        @pl.when(me > 0)
        def _():
            block_right(c).wait_recv()

        @pl.when(me < n - 1)
        def _():
            block_left(c).wait_recv()

        at = block_at(c)
        shape = (bsize, ROWS, LANES)
        moved = advect(l0[at, :].reshape(shape), left[at, :].reshape(shape), right[at, :].reshape(shape))
        names = pl.ds(pl.multiple_of(c * bsize, bsize), bsize)
        result = scol[names, :][:, None, :] * moved - gcol[names, :][:, None, :] * air_out[None]
        out[at, :] = result.reshape(bl, LANES)
        out_copy(c).start()

    plain[8].wait()
    for x in range(2):
        ground = out[pl.ds(x, species, stride=ROWS), :]
        grad[pl.ds(x, emis.shape[0], stride=2), :] = jnp.dot(
            emis[...], ground, precision=lax.Precision.HIGHEST, preferred_element_type=F32
        )
    grad_copy = pltpu.make_async_copy(grad, grad_h, out_sem.at[nblocks])
    grad_copy.start()

    @pl.loop(0, nblocks)
    def _(c):
        @pl.when(me < n - 1)
        def _():
            block_right(c).wait_send()

        @pl.when(me > 0)
        def _():
            block_left(c).wait_send()

        out_copy(c).wait()

    @pl.when(me < n - 1)
    def _():
        to_right(small, small_l, ssem.at[0], ssem.at[1]).wait_send()

    @pl.when(me > 0)
    def _():
        to_left(small, small_r, ssem.at[2], ssem.at[3]).wait_send()

    @pl.loop(1, n)
    def _(k):
        stat_copy(k).wait_send()

    grad_copy.wait()


def body(
    lam_in, conc, jac_diag, jac_off, block_rows, block_cols, active, courant, kz, airmass, target, emis_map
):
    species, levels, width, ny = lam_in.shape
    n = lax.axis_size("col")
    nblocks, bsize = jac_diag.shape[:2]
    slots = jac_off.shape[0]
    cells = levels * width * ny * n
    fields = emis_map.shape[0]

    def flat(x):
        return x.reshape(-1, ny)

    operands = [
        flat(lam_in), flat(conc), flat(jac_diag), flat(jac_off), flat(block_rows), flat(block_cols),
        flat(active), flat(courant), kz, flat(airmass), target.reshape(1, species), emis_map,
    ]
    big = (species * ROWS, ny)
    held = [pltpu.VMEM(x.shape, x.dtype) for x in operands]
    dma = pltpu.SemaphoreType.DMA
    out, grad = pl.pallas_call(
        functools.partial(kernel, nblocks, bsize, slots, levels, cells, n),
        out_shape=(
            jax.ShapeDtypeStruct(big, F32),
            jax.ShapeDtypeStruct((fields * width, ny), F32),
        ),
        in_specs=[pl.BlockSpec(memory_space=pl.ANY)] * len(operands),
        out_specs=(pl.BlockSpec(memory_space=pl.ANY),) * 2,
        scratch_shapes=held
        + [
            pltpu.VMEM(big, F32), pltpu.VMEM(big, F32), pltpu.VMEM(big, F32), pltpu.VMEM(big, F32),
            pltpu.VMEM((fields * width, ny), F32),
            pltpu.VMEM((slots, bsize, ROWS, ny), F32),
            pltpu.VMEM((levels, ROWS, ny), F32),
            pltpu.VMEM((24, ny), F32), pltpu.VMEM((24, ny), F32), pltpu.VMEM((24, ny), F32),
            pltpu.VMEM((2, species, ny), F32),
            pltpu.VMEM((4, ny), F32), pltpu.VMEM((n, 4, ny), F32),
            pltpu.VMEM((species, ny), F32), pltpu.VMEM((species, ny), F32),
            dma((10,)), dma((slots,)), dma((nblocks,)), dma((nblocks + 1,)),
            dma((nblocks,)), dma((nblocks,)), dma((nblocks,)), dma((nblocks,)),
            dma((4,)), dma((n,)), dma((n,)),
        ],
        compiler_params=pltpu.CompilerParams(
            collective_id=0, has_side_effects=True, vmem_limit_bytes=60 * 2**20
        ),
        cost_estimate=pl.CostEstimate(flops=8_000_000, bytes_accessed=10_000_000, transcendentals=0),
    )(*operands)
    return out.reshape(lam_in.shape), grad.reshape(fields, width, ny)


def solution(mesh):
    return jax.shard_map(
        body,
        mesh=mesh,
        in_specs=(
            P("grp", None, "col", None),
            P("grp", None, "col", None),
            P("grp", None, None, None, "col", None),
            P("grp", None, None, None, "col", None),
            P("grp", None, "col", None),
            P("grp", None, "col", None),
            P("grp", "col", None),
            P(None, "grp", "col", None),
            P("grp", "col", None),
            P("grp", "col", None),
            P("grp"),
            P(),
        ),
        out_specs=(P("grp", None, "col", None), P("grp", "col", None)),
        check_vma=False,
    )
```

```python
import functools

import jax
import jax.numpy as jnp
from jax import lax
from jax.experimental import pallas as pl
from jax.experimental.pallas import tpu as pltpu
from jax.sharding import PartitionSpec as P

ADV = 2
ROWS = 8
LANES = 128
F32 = jnp.float32


def inverse_levels(kz):
    levels = len(kz) + 1
    diag = []
    for lev in range(levels):
        value = jnp.ones_like(kz[0])
        if lev > 0:
            value = value + kz[lev - 1]
        if lev < levels - 1:
            value = value + kz[lev]
        diag.append(value)
    cprime, recip = [], []
    for lev in range(levels):
        denom = diag[lev]
        if lev > 0:
            denom = denom + kz[lev - 1] * cprime[lev - 1]
        recip.append(1.0 / denom)
        cprime.append(-kz[lev] * recip[lev] if lev < levels - 1 else None)
    result = [[None] * levels for _ in range(levels)]
    for unit in range(levels):
        dprime = []
        for lev in range(levels):
            if lev < unit:
                dprime.append(jnp.zeros_like(kz[0]))
            elif lev == unit:
                dprime.append(recip[lev])
            else:
                dprime.append(kz[lev - 1] * dprime[lev - 1] * recip[lev])
        solved = dprime[levels - 1]
        result[levels - 1][unit] = solved
        for lev in range(levels - 2, -1, -1):
            solved = dprime[lev] - cprime[lev] * solved
            result[lev][unit] = solved
    return result


def up(x):
    return pltpu.roll(x, ROWS - 1, x.ndim - 2)


def down(x):
    return pltpu.roll(x, 1, x.ndim - 2)


def kernel(
    nblocks, bsize, slots, levels, cells, n,
    lam_h, conc_h, jd_h, jo_h, rows_h, cols_h, act_h, cour_h, kz_h, air_h, target_h,
    out_h,
    lam, conc, jd, jo, rows, cols, act, cour, kz, air, target,
    l0, left, right, contrib, solve, small, small_l, small_r,
    part, stat, stats, scol, gcol,
    in_sem, jo_sem, jd_sem, send_r, send_l, recv_l, recv_r, ssem, stat_send, stat_recv,
):
    me = lax.axis_index("col")
    species = nblocks * bsize
    bl = bsize * ROWS
    step = bsize * bl

    def peer(k):
        return lax.rem(me + k, n)

    barrier = pltpu.get_barrier_semaphore()

    @pl.loop(1, n)
    def _(k):
        pl.semaphore_signal(
            barrier, inc=1, device_id={"col": peer(k)}, device_id_type=pl.DeviceIdType.MESH
        )

    plain = [
        pltpu.make_async_copy(src, dst, in_sem.at[k])
        for k, (src, dst) in enumerate(
            [
                (lam_h, lam), (rows_h, rows), (cols_h, cols), (act_h, act), (kz_h, kz),
                (cour_h, cour), (air_h, air), (target_h, target), (conc_h, conc),
            ]
        )
    ]

    def jo_copy(p):
        at = pl.ds(pl.multiple_of(p * step, step), step)
        return pltpu.make_async_copy(jo_h.at[at], jo.at[at], jo_sem.at[p])

    def jd_copy(c):
        at = pl.ds(pl.multiple_of(c * step, step), step)
        return pltpu.make_async_copy(jd_h.at[at], jd.at[at], jd_sem.at[c])

    for copy in plain[:8]:
        copy.start()
    for p in range(slots):
        jo_copy(p).start()
    for c in range(nblocks):
        jd_copy(c).start()
        if c == 0:
            plain[8].start()

    @pl.when(me == 0)
    def _():
        left[...] = jnp.zeros_like(left)
        small_l[...] = jnp.zeros_like(small_l)

    @pl.when(me == n - 1)
    def _():
        right[...] = jnp.zeros_like(right)
        small_r[...] = jnp.zeros_like(small_r)

    for copy in plain[1:8]:
        copy.wait()

    kzs = [kz[lev] for lev in range(levels - 1)]
    inverse = inverse_levels(kzs)
    for shift in range(levels):
        for lev in range(levels):
            solve[shift, 2 * lev : 2 * lev + 2, :] = inverse[lev][(lev - shift) % levels]

    def solve_levels(x):
        total = x * solve[0]
        for shift in range(1, levels):
            total = total + pltpu.roll(x, 2 * shift, x.ndim - 2) * solve[shift]
        return total

    small[0:8, :] = cour[0:8, :]
    small[8:16, :] = cour[8:16, :]
    small[16:24, :] = solve_levels(air[...])

    plain[0].wait()

    @pl.loop(0, slots)
    def _(p):
        live = act[...] > p
        want = jnp.where(live, rows[pl.ds(pl.multiple_of(p * ROWS, ROWS), ROWS), :], -1)
        chosen = jnp.zeros((bsize, ROWS, LANES), F32)
        for b in range(nblocks):
            block = lam[b * bl : (b + 1) * bl, :].reshape(bsize, ROWS, LANES)
            chosen = jnp.where((want == b)[None], block, chosen)
        jo_copy(p).wait()
        acc = jnp.zeros((bsize, ROWS, LANES), F32)
        for i in range(bsize):
            at = pl.ds(pl.multiple_of(p * step + i * bl, bl), bl)
            acc = acc + jo[at, :].astype(F32).reshape(bsize, ROWS, LANES) * chosen[i][None]
        contrib[p] = acc

    pl.semaphore_wait(barrier, n - 1)

    def to_right(src, dst, ssem_, rsem):
        return pltpu.make_async_remote_copy(
            src_ref=src, dst_ref=dst, send_sem=ssem_, recv_sem=rsem,
            device_id={"col": jnp.minimum(me + 1, n - 1)}, device_id_type=pl.DeviceIdType.MESH,
        )

    def to_left(src, dst, ssem_, rsem):
        return pltpu.make_async_remote_copy(
            src_ref=src, dst_ref=dst, send_sem=ssem_, recv_sem=rsem,
            device_id={"col": jnp.maximum(me - 1, 0)}, device_id_type=pl.DeviceIdType.MESH,
        )

    def block_at(c):
        return pl.ds(pl.multiple_of(c * bl, bl), bl)

    def block_right(c):
        return to_right(l0.at[block_at(c)], left.at[block_at(c)], send_r.at[c], recv_l.at[c])

    def block_left(c):
        return to_left(l0.at[block_at(c)], right.at[block_at(c)], send_l.at[c], recv_r.at[c])

    early = nblocks // 2

    def send_block(c):
        @pl.when(me < n - 1)
        def _():
            block_right(c).start()

        @pl.when(me > 0)
        def _():
            block_left(c).start()

    small_right = to_right(small, small_l, ssem.at[0], ssem.at[1])
    small_left = to_left(small, small_r, ssem.at[2], ssem.at[3])

    @pl.when(me < n - 1)
    def _():
        small_right.start()

    @pl.when(me > 0)
    def _():
        small_left.start()

    plain[8].wait()

    @pl.loop(0, nblocks)
    def _(c):
        block = lam[block_at(c), :].reshape(bsize, ROWS, LANES)
        jd_copy(c).wait()
        acc = block
        for i in range(bsize):
            at = pl.ds(pl.multiple_of(c * step + i * bl, bl), bl)
            acc = acc + jd[at, :].astype(F32).reshape(bsize, ROWS, LANES) * block[i][None]
        for p in range(slots):
            place = cols[p * ROWS : (p + 1) * ROWS, :] == c
            acc = acc + jnp.where(place[None], contrib[p], 0.0)
        l0[block_at(c), :] = solve_levels(acc).reshape(bl, LANES)

        @pl.when(c < early)
        def _():
            send_block(c)

        amount = conc[block_at(c), :].reshape(bsize, ROWS, LANES)
        at = pl.ds(pl.multiple_of(c * bsize, bsize), bsize)
        part[0, at, :] = jnp.sum(amount * air[...][None], axis=1)
        part[1, at, :] = jnp.sum(amount * acc, axis=1)

    tail = species - LANES
    for which in range(2):
        for half, first in enumerate((0, tail)):
            square = part[which, first : first + LANES, :]
            stat[2 * which + half : 2 * which + half + 1, :] = jnp.sum(
                square.T, axis=0, keepdims=True
            )

    def stat_copy(k):
        return pltpu.make_async_remote_copy(
            src_ref=stat, dst_ref=stats.at[me], send_sem=stat_send.at[k], recv_sem=stat_recv.at[me],
            device_id={"col": peer(k)}, device_id_type=pl.DeviceIdType.MESH,
        )

    def stat_from(k):
        source = lax.rem(me + n - k, n)
        return source, pltpu.make_async_remote_copy(
            src_ref=stat, dst_ref=stats.at[source], send_sem=stat_send.at[k],
            recv_sem=stat_recv.at[source],
            device_id={"col": peer(k)}, device_id_type=pl.DeviceIdType.MESH,
        )

    @pl.loop(1, n)
    def _(k):
        stat_copy(k).start()

    @pl.loop(early, nblocks)
    def _(c):
        send_block(c)

    @pl.when(me > 0)
    def _():
        to_right(small, small_l, ssem.at[0], ssem.at[1]).wait_recv()

    @pl.when(me < n - 1)
    def _():
        to_left(small, small_r, ssem.at[2], ssem.at[3]).wait_recv()

    even = lax.rem(lax.broadcasted_iota(jnp.int32, (ROWS, LANES), 0), 2) == 0

    def swap(x):
        return jnp.where(even, up(x), down(x))

    a, b = small[0:8, :], small[8:16, :]
    c = 1.0 - a - b
    al, bl_ = small_l[0:8, :], small_l[8:16, :]
    cl = 1.0 - al - bl_
    ar, br = small_r[0:8, :], small_r[8:16, :]
    cr = 1.0 - ar - br
    own_same = c * c + jnp.where(even, b * swap(al) + a * swap(b), b * swap(a) + a * swap(br))
    own_swap = jnp.where(even, a, b) * (c + swap(c))
    left_same = b * jnp.where(even, swap(bl_), swap(b))
    left_up = jnp.where(even, b * (c + swap(cl)), 0.0)
    right_same = a * jnp.where(even, swap(a), swap(ar))
    right_down = jnp.where(even, 0.0, a * (c + swap(cr)))

    def advect(mid, lt, rt):
        return (
            own_same * mid
            + own_swap * jnp.where(even, up(mid), down(mid))
            + left_same * lt
            + left_up * up(lt)
            + right_same * rt
            + right_down * down(rt)
        )

    air_out = advect(small[16:24, :], small_l[16:24, :], small_r[16:24, :])

    def add_stat(k, total):
        source, copy = stat_from(k)
        copy.wait_recv()
        return total + stats[source]

    total = lax.fori_loop(1, n, add_stat, stat[...])
    for half, first in enumerate((0, tail)):
        mass = total[half : half + 1, :]
        quad = total[2 + half : 3 + half, :]
        scale = target[:, first : first + LANES] * float(cells) / mass
        gain = scale * quad / mass
        scol[first : first + LANES, :] = jnp.broadcast_to(scale, (LANES, LANES)).T
        gcol[first : first + LANES, :] = jnp.broadcast_to(gain, (LANES, LANES)).T

    @pl.loop(0, nblocks)
    def _(c):
        @pl.when(me > 0)
        def _():
            block_right(c).wait_recv()

        @pl.when(me < n - 1)
        def _():
            block_left(c).wait_recv()

        at = block_at(c)
        shape = (bsize, ROWS, LANES)
        moved = advect(l0[at, :].reshape(shape), left[at, :].reshape(shape), right[at, :].reshape(shape))
        names = pl.ds(pl.multiple_of(c * bsize, bsize), bsize)
        result = scol[names, :][:, None, :] * moved - gcol[names, :][:, None, :] * air_out[None]
        out_h[at, :] = result.reshape(bl, LANES)

    @pl.loop(0, nblocks)
    def _(c):
        @pl.when(me < n - 1)
        def _():
            block_right(c).wait_send()

        @pl.when(me > 0)
        def _():
            block_left(c).wait_send()

    @pl.when(me < n - 1)
    def _():
        to_right(small, small_l, ssem.at[0], ssem.at[1]).wait_send()

    @pl.when(me > 0)
    def _():
        to_left(small, small_r, ssem.at[2], ssem.at[3]).wait_send()

    @pl.loop(1, n)
    def _(k):
        stat_copy(k).wait_send()


def finish(nblocks, value, emis, out_h, grad_h, grad, sem):
    species, fields = emis.shape[1], emis.shape[0]
    lam_copy = pltpu.make_async_copy(value, out_h, sem.at[0])
    lam_copy.start()
    for x in range(2):
        ground = value[pl.ds(x, species, stride=ROWS), :]
        grad[pl.ds(x, fields, stride=2), :] = jnp.dot(
            emis[...], ground, precision=lax.Precision.HIGHEST, preferred_element_type=F32
        )
    grad_copy = pltpu.make_async_copy(grad, grad_h, sem.at[1])
    grad_copy.start()
    lam_copy.wait()
    grad_copy.wait()


def body(
    lam_in, conc, jac_diag, jac_off, block_rows, block_cols, active, courant, kz, airmass, target, emis_map
):
    species, levels, width, ny = lam_in.shape
    n = lax.axis_size("col")
    nblocks, bsize = jac_diag.shape[:2]
    slots = jac_off.shape[0]
    cells = levels * width * ny * n
    fields = emis_map.shape[0]

    def flat(x):
        return x.reshape(-1, ny)

    operands = [
        flat(lam_in), flat(conc), flat(jac_diag), flat(jac_off), flat(block_rows), flat(block_cols),
        flat(active), flat(courant), kz, flat(airmass), target.reshape(1, species),
    ]
    big = (species * ROWS, ny)
    held = [pltpu.VMEM(x.shape, x.dtype) for x in operands]
    dma = pltpu.SemaphoreType.DMA
    whole = pl.BlockSpec(memory_space=pltpu.VMEM)
    value = pl.pallas_call(
        functools.partial(kernel, nblocks, bsize, slots, levels, cells, n),
        out_shape=pltpu.VMEM(big, F32),
        in_specs=[pl.BlockSpec(memory_space=pltpu.HBM)] * len(operands),
        out_specs=whole,
        scratch_shapes=held
        + [
            pltpu.VMEM(big, F32), pltpu.VMEM(big, F32), pltpu.VMEM(big, F32),
            pltpu.VMEM((slots, bsize, ROWS, ny), F32),
            pltpu.VMEM((levels, ROWS, ny), F32),
            pltpu.VMEM((24, ny), F32), pltpu.VMEM((24, ny), F32), pltpu.VMEM((24, ny), F32),
            pltpu.VMEM((2, species, ny), F32),
            pltpu.VMEM((4, ny), F32), pltpu.VMEM((n, 4, ny), F32),
            pltpu.VMEM((species, ny), F32), pltpu.VMEM((species, ny), F32),
            dma((9,)), dma((slots,)), dma((nblocks,)),
            dma((nblocks,)), dma((nblocks,)), dma((nblocks,)), dma((nblocks,)),
            dma((4,)), dma((n,)), dma((n,)),
        ],
        compiler_params=pltpu.CompilerParams(
            collective_id=0, has_side_effects=True, vmem_limit_bytes=60 * 2**20
        ),
        cost_estimate=pl.CostEstimate(flops=8_000_000, bytes_accessed=10_000_000, transcendentals=0),
    )(*operands)
    hbm = pl.BlockSpec(memory_space=pltpu.HBM)
    out, grad = pl.pallas_call(
        functools.partial(finish, nblocks),
        out_shape=(
            jax.ShapeDtypeStruct(big, F32),
            jax.ShapeDtypeStruct((fields * width, ny), F32),
        ),
        in_specs=[whole, whole],
        out_specs=(hbm, hbm),
        scratch_shapes=[pltpu.VMEM((fields * width, ny), F32), dma((2,))],
        compiler_params=pltpu.CompilerParams(vmem_limit_bytes=4 * 2**20),
        cost_estimate=pl.CostEstimate(flops=6_000_000, bytes_accessed=1_400_000, transcendentals=0),
    )(value, emis_map)
    return out.reshape(lam_in.shape), grad.reshape(fields, width, ny)


def solution(mesh):
    return jax.shard_map(
        body,
        mesh=mesh,
        in_specs=(
            P("grp", None, "col", None),
            P("grp", None, "col", None),
            P("grp", None, None, None, "col", None),
            P("grp", None, None, None, "col", None),
            P("grp", None, "col", None),
            P("grp", None, "col", None),
            P("grp", "col", None),
            P(None, "grp", "col", None),
            P("grp", "col", None),
            P("grp", "col", None),
            P("grp"),
            P(),
        ),
        out_specs=(P("grp", None, "col", None), P("grp", "col", None)),
        check_vma=False,
    )
```

```python
import functools

import jax
import jax.numpy as jnp
from jax import lax
from jax.experimental import pallas as pl
from jax.experimental.pallas import tpu as pltpu
from jax.sharding import PartitionSpec as P

ADV = 2
ROWS = 8
LANES = 128
F32 = jnp.float32


def inverse_levels(kz):
    levels = len(kz) + 1
    diag = []
    for lev in range(levels):
        value = jnp.ones_like(kz[0])
        if lev > 0:
            value = value + kz[lev - 1]
        if lev < levels - 1:
            value = value + kz[lev]
        diag.append(value)
    cprime, recip = [], []
    for lev in range(levels):
        denom = diag[lev]
        if lev > 0:
            denom = denom + kz[lev - 1] * cprime[lev - 1]
        recip.append(1.0 / denom)
        cprime.append(-kz[lev] * recip[lev] if lev < levels - 1 else None)
    result = [[None] * levels for _ in range(levels)]
    for unit in range(levels):
        dprime = []
        for lev in range(levels):
            if lev < unit:
                dprime.append(jnp.zeros_like(kz[0]))
            elif lev == unit:
                dprime.append(recip[lev])
            else:
                dprime.append(kz[lev - 1] * dprime[lev - 1] * recip[lev])
        solved = dprime[levels - 1]
        result[levels - 1][unit] = solved
        for lev in range(levels - 2, -1, -1):
            solved = dprime[lev] - cprime[lev] * solved
            result[lev][unit] = solved
    return result


def up(x):
    return pltpu.roll(x, ROWS - 1, x.ndim - 2)


def down(x):
    return pltpu.roll(x, 1, x.ndim - 2)


def kernel(
    nblocks, bsize, slots, levels, cells, n,
    lam_h, conc_h, jd_h, jo_h, rows_h, cols_h, act_h, cour_h, kz_h, air_h, target_h,
    out_h,
    lam, conc, jd, jo, rows, cols, act, cour, kz, air, target,
    l0, left, right, contrib, solve, small, small_l, small_r,
    part, stat, stats, scol, gcol,
    relayed, in_sem, jo_sem, jd_sem, send_r, send_l, recv_l, recv_r, relay_send, relay_recv, ssem, stat_send, stat_recv,
):
    me = lax.axis_index("col")
    species = nblocks * bsize
    bl = bsize * ROWS
    step = bsize * bl

    def peer(k):
        return lax.rem(me + k, n)

    barrier = pltpu.get_barrier_semaphore()

    @pl.loop(1, n)
    def _(k):
        pl.semaphore_signal(
            barrier, inc=1, device_id={"col": peer(k)}, device_id_type=pl.DeviceIdType.MESH
        )

    plain = [
        pltpu.make_async_copy(src, dst, in_sem.at[k])
        for k, (src, dst) in enumerate(
            [
                (lam_h, lam), (rows_h, rows), (cols_h, cols), (act_h, act), (kz_h, kz),
                (cour_h, cour), (air_h, air), (target_h, target), (conc_h, conc),
            ]
        )
    ]

    def jo_copy(p):
        at = pl.ds(pl.multiple_of(p * step, step), step)
        return pltpu.make_async_copy(jo_h.at[at], jo.at[at], jo_sem.at[p])

    def jd_copy(c):
        at = pl.ds(pl.multiple_of(c * step, step), step)
        return pltpu.make_async_copy(jd_h.at[at], jd.at[at], jd_sem.at[c])

    for copy in plain[:8]:
        copy.start()
    for p in range(slots):
        jo_copy(p).start()
    for c in range(nblocks):
        jd_copy(c).start()
        if c == 0:
            plain[8].start()

    @pl.when(me == 0)
    def _():
        left[...] = jnp.zeros_like(left)
        small_l[...] = jnp.zeros_like(small_l)

    @pl.when(me == n - 1)
    def _():
        right[...] = jnp.zeros_like(right)
        small_r[...] = jnp.zeros_like(small_r)

    for copy in plain[1:8]:
        copy.wait()

    kzs = [kz[lev] for lev in range(levels - 1)]
    inverse = inverse_levels(kzs)
    for shift in range(levels):
        for lev in range(levels):
            solve[shift, 2 * lev : 2 * lev + 2, :] = inverse[lev][(lev - shift) % levels]

    def solve_levels(x):
        total = x * solve[0]
        for shift in range(1, levels):
            total = total + pltpu.roll(x, 2 * shift, x.ndim - 2) * solve[shift]
        return total

    small[0:8, :] = cour[0:8, :]
    small[8:16, :] = cour[8:16, :]
    small[16:24, :] = solve_levels(air[...])

    plain[0].wait()

    @pl.loop(0, slots)
    def _(p):
        live = act[...] > p
        want = jnp.where(live, rows[pl.ds(pl.multiple_of(p * ROWS, ROWS), ROWS), :], -1)
        chosen = jnp.zeros((bsize, ROWS, LANES), F32)
        for b in range(nblocks):
            block = lam[b * bl : (b + 1) * bl, :].reshape(bsize, ROWS, LANES)
            chosen = jnp.where((want == b)[None], block, chosen)
        jo_copy(p).wait()
        acc = jnp.zeros((bsize, ROWS, LANES), F32)
        for i in range(bsize):
            at = pl.ds(pl.multiple_of(p * step + i * bl, bl), bl)
            acc = acc + jo[at, :].astype(F32).reshape(bsize, ROWS, LANES) * chosen[i][None]
        contrib[p] = acc

    pl.semaphore_wait(barrier, n - 1)

    def to_right(src, dst, ssem_, rsem):
        return pltpu.make_async_remote_copy(
            src_ref=src, dst_ref=dst, send_sem=ssem_, recv_sem=rsem,
            device_id={"col": jnp.minimum(me + 1, n - 1)}, device_id_type=pl.DeviceIdType.MESH,
        )

    def to_left(src, dst, ssem_, rsem):
        return pltpu.make_async_remote_copy(
            src_ref=src, dst_ref=dst, send_sem=ssem_, recv_sem=rsem,
            device_id={"col": jnp.maximum(me - 1, 0)}, device_id_type=pl.DeviceIdType.MESH,
        )

    def block_at(c):
        return pl.ds(pl.multiple_of(c * bl, bl), bl)

    def block_right(c):
        return to_right(l0.at[block_at(c)], left.at[block_at(c)], send_r.at[c], recv_l.at[c])

    def block_left(c):
        return to_left(l0.at[block_at(c)], right.at[block_at(c)], send_l.at[c], recv_r.at[c])

    early = nblocks // 2

    relaying = n == 16
    place4, plane = lax.rem(me, 4), me // 4
    relay_until = nblocks - 4
    from_left_flow = (place4 == 0) & (plane > 0)
    from_right_flow = (place4 == 3) & (plane < 3)
    relay_left = (place4 == 2) & (plane > 0)
    relay_right = (place4 == 1) & (plane < 3)
    share = jnp.where(place4 % 2 == 0, 2 * plane, 6 - 2 * plane)

    def takes_relay(c):
        return (c < relay_until) & (lax.rem(c * share, relay_until) < share)

    def to_relay(c, offset, sems):
        return pltpu.make_async_remote_copy(
            src_ref=l0.at[block_at(c)], dst_ref=relayed.at[block_at(c)],
            send_sem=sems.at[c], recv_sem=relay_recv.at[c],
            device_id={"col": lax.rem(me + n + offset, n)}, device_id_type=pl.DeviceIdType.MESH,
        )

    def onward(c, offset, dst, sems):
        return pltpu.make_async_remote_copy(
            src_ref=relayed.at[block_at(c)], dst_ref=dst.at[block_at(c)],
            send_sem=relay_send.at[c], recv_sem=sems.at[c],
            device_id={"col": lax.rem(me + n + offset, n)}, device_id_type=pl.DeviceIdType.MESH,
        )

    def forward(c):
        @pl.when(relay_left & takes_relay(c))
        def _():
            to_relay(c, 2, send_l).wait_recv()
            onward(c, -3, right, recv_r).start()

        @pl.when(relay_right & takes_relay(c))
        def _():
            to_relay(c, -2, send_r).wait_recv()
            onward(c, 3, left, recv_l).start()

    def send_block(c):
        if relaying:
            detour_right = from_right_flow & takes_relay(c)
            detour_left = from_left_flow & takes_relay(c)

            @pl.when(detour_right)
            def _():
                to_relay(c, -2, send_r).start()

            @pl.when(detour_left)
            def _():
                to_relay(c, 2, send_l).start()

            direct_right = (me < n - 1) & jnp.logical_not(detour_right)
            direct_left = (me > 0) & jnp.logical_not(detour_left)
        else:
            direct_right, direct_left = me < n - 1, me > 0

        @pl.when(direct_right)
        def _():
            block_right(c).start()

        @pl.when(direct_left)
        def _():
            block_left(c).start()

    small_right = to_right(small, small_l, ssem.at[0], ssem.at[1])
    small_left = to_left(small, small_r, ssem.at[2], ssem.at[3])

    @pl.when(me < n - 1)
    def _():
        small_right.start()

    @pl.when(me > 0)
    def _():
        small_left.start()

    plain[8].wait()

    @pl.loop(0, nblocks)
    def _(c):
        block = lam[block_at(c), :].reshape(bsize, ROWS, LANES)
        jd_copy(c).wait()
        acc = block
        for i in range(bsize):
            at = pl.ds(pl.multiple_of(c * step + i * bl, bl), bl)
            acc = acc + jd[at, :].astype(F32).reshape(bsize, ROWS, LANES) * block[i][None]
        for p in range(slots):
            place = cols[p * ROWS : (p + 1) * ROWS, :] == c
            acc = acc + jnp.where(place[None], contrib[p], 0.0)
        l0[block_at(c), :] = solve_levels(acc).reshape(bl, LANES)

        @pl.when(c < early)
        def _():
            send_block(c)

        amount = conc[block_at(c), :].reshape(bsize, ROWS, LANES)
        at = pl.ds(pl.multiple_of(c * bsize, bsize), bsize)
        part[0, at, :] = jnp.sum(amount * air[...][None], axis=1)
        part[1, at, :] = jnp.sum(amount * acc, axis=1)

    tail = species - LANES
    for which in range(2):
        for half, first in enumerate((0, tail)):
            square = part[which, first : first + LANES, :]
            stat[2 * which + half : 2 * which + half + 1, :] = jnp.sum(
                square.T, axis=0, keepdims=True
            )

    def stat_copy(k):
        return pltpu.make_async_remote_copy(
            src_ref=stat, dst_ref=stats.at[me], send_sem=stat_send.at[k], recv_sem=stat_recv.at[me],
            device_id={"col": peer(k)}, device_id_type=pl.DeviceIdType.MESH,
        )

    def stat_from(k):
        source = lax.rem(me + n - k, n)
        return source, pltpu.make_async_remote_copy(
            src_ref=stat, dst_ref=stats.at[source], send_sem=stat_send.at[k],
            recv_sem=stat_recv.at[source],
            device_id={"col": peer(k)}, device_id_type=pl.DeviceIdType.MESH,
        )

    @pl.loop(1, n)
    def _(k):
        stat_copy(k).start()

    @pl.loop(early, nblocks)
    def _(c):
        send_block(c)

    if relaying:

        @pl.loop(0, early)
        def _(c):
            forward(c)

    @pl.when(me > 0)
    def _():
        to_right(small, small_l, ssem.at[0], ssem.at[1]).wait_recv()

    @pl.when(me < n - 1)
    def _():
        to_left(small, small_r, ssem.at[2], ssem.at[3]).wait_recv()

    even = lax.rem(lax.broadcasted_iota(jnp.int32, (ROWS, LANES), 0), 2) == 0

    def swap(x):
        return jnp.where(even, up(x), down(x))

    a, b = small[0:8, :], small[8:16, :]
    c = 1.0 - a - b
    al, bl_ = small_l[0:8, :], small_l[8:16, :]
    cl = 1.0 - al - bl_
    ar, br = small_r[0:8, :], small_r[8:16, :]
    cr = 1.0 - ar - br
    own_same = c * c + jnp.where(even, b * swap(al) + a * swap(b), b * swap(a) + a * swap(br))
    own_swap = jnp.where(even, a, b) * (c + swap(c))
    left_same = b * jnp.where(even, swap(bl_), swap(b))
    left_up = jnp.where(even, b * (c + swap(cl)), 0.0)
    right_same = a * jnp.where(even, swap(a), swap(ar))
    right_down = jnp.where(even, 0.0, a * (c + swap(cr)))

    def advect(mid, lt, rt):
        return (
            own_same * mid
            + own_swap * jnp.where(even, up(mid), down(mid))
            + left_same * lt
            + left_up * up(lt)
            + right_same * rt
            + right_down * down(rt)
        )

    air_out = advect(small[16:24, :], small_l[16:24, :], small_r[16:24, :])

    def add_stat(k, total):
        source, copy = stat_from(k)
        copy.wait_recv()
        return total + stats[source]

    total = lax.fori_loop(1, n, add_stat, stat[...])
    for half, first in enumerate((0, tail)):
        mass = total[half : half + 1, :]
        quad = total[2 + half : 3 + half, :]
        scale = target[:, first : first + LANES] * float(cells) / mass
        gain = scale * quad / mass
        scol[first : first + LANES, :] = jnp.broadcast_to(scale, (LANES, LANES)).T
        gcol[first : first + LANES, :] = jnp.broadcast_to(gain, (LANES, LANES)).T

    @pl.loop(0, nblocks)
    def _(c):
        if relaying:

            @pl.when(c < relay_until - early)
            def _():
                forward(c + early)

        @pl.when(me > 0)
        def _():
            block_right(c).wait_recv()

        @pl.when(me < n - 1)
        def _():
            block_left(c).wait_recv()

        at = block_at(c)
        shape = (bsize, ROWS, LANES)
        moved = advect(l0[at, :].reshape(shape), left[at, :].reshape(shape), right[at, :].reshape(shape))
        names = pl.ds(pl.multiple_of(c * bsize, bsize), bsize)
        result = scol[names, :][:, None, :] * moved - gcol[names, :][:, None, :] * air_out[None]
        out_h[at, :] = result.reshape(bl, LANES)

    @pl.loop(0, nblocks)
    def _(c):
        @pl.when(me < n - 1)
        def _():
            block_right(c).wait_send()

        @pl.when(me > 0)
        def _():
            block_left(c).wait_send()

        if relaying:

            @pl.when((relay_left | relay_right) & takes_relay(c))
            def _():
                onward(c, 3, left, recv_l).wait_send()

    @pl.when(me < n - 1)
    def _():
        to_right(small, small_l, ssem.at[0], ssem.at[1]).wait_send()

    @pl.when(me > 0)
    def _():
        to_left(small, small_r, ssem.at[2], ssem.at[3]).wait_send()

    @pl.loop(1, n)
    def _(k):
        stat_copy(k).wait_send()


def finish(nblocks, value, emis, out_h, grad_h, grad, sem):
    species, fields = emis.shape[1], emis.shape[0]
    lam_copy = pltpu.make_async_copy(value, out_h, sem.at[0])
    lam_copy.start()
    for x in range(2):
        ground = value[pl.ds(x, species, stride=ROWS), :]
        grad[pl.ds(x, fields, stride=2), :] = jnp.dot(
            emis[...], ground, precision=lax.Precision.HIGHEST, preferred_element_type=F32
        )
    grad_copy = pltpu.make_async_copy(grad, grad_h, sem.at[1])
    grad_copy.start()
    lam_copy.wait()
    grad_copy.wait()


def body(
    lam_in, conc, jac_diag, jac_off, block_rows, block_cols, active, courant, kz, airmass, target, emis_map
):
    species, levels, width, ny = lam_in.shape
    n = lax.axis_size("col")
    nblocks, bsize = jac_diag.shape[:2]
    slots = jac_off.shape[0]
    cells = levels * width * ny * n
    fields = emis_map.shape[0]

    def flat(x):
        return x.reshape(-1, ny)

    operands = [
        flat(lam_in), flat(conc), flat(jac_diag), flat(jac_off), flat(block_rows), flat(block_cols),
        flat(active), flat(courant), kz, flat(airmass), target.reshape(1, species),
    ]
    big = (species * ROWS, ny)
    held = [pltpu.VMEM(x.shape, x.dtype) for x in operands]
    dma = pltpu.SemaphoreType.DMA
    whole = pl.BlockSpec(memory_space=pltpu.VMEM)
    value = pl.pallas_call(
        functools.partial(kernel, nblocks, bsize, slots, levels, cells, n),
        out_shape=pltpu.VMEM(big, F32),
        in_specs=[pl.BlockSpec(memory_space=pltpu.HBM)] * len(operands),
        out_specs=whole,
        scratch_shapes=held
        + [
            pltpu.VMEM(big, F32), pltpu.VMEM(big, F32), pltpu.VMEM(big, F32),
            pltpu.VMEM((slots, bsize, ROWS, ny), F32),
            pltpu.VMEM((levels, ROWS, ny), F32),
            pltpu.VMEM((24, ny), F32), pltpu.VMEM((24, ny), F32), pltpu.VMEM((24, ny), F32),
            pltpu.VMEM((2, species, ny), F32),
            pltpu.VMEM((4, ny), F32), pltpu.VMEM((n, 4, ny), F32),
            pltpu.VMEM((species, ny), F32), pltpu.VMEM((species, ny), F32),
            pltpu.VMEM(big, F32),
            dma((9,)), dma((slots,)), dma((nblocks,)),
            dma((nblocks,)), dma((nblocks,)), dma((nblocks,)), dma((nblocks,)),
            dma((nblocks,)), dma((nblocks,)), dma((4,)), dma((n,)), dma((n,)),
        ],
        compiler_params=pltpu.CompilerParams(
            collective_id=0, has_side_effects=True, vmem_limit_bytes=60 * 2**20
        ),
        cost_estimate=pl.CostEstimate(flops=8_000_000, bytes_accessed=10_000_000, transcendentals=0),
    )(*operands)
    hbm = pl.BlockSpec(memory_space=pltpu.HBM)
    out, grad = pl.pallas_call(
        functools.partial(finish, nblocks),
        out_shape=(
            jax.ShapeDtypeStruct(big, F32),
            jax.ShapeDtypeStruct((fields * width, ny), F32),
        ),
        in_specs=[whole, whole],
        out_specs=(hbm, hbm),
        scratch_shapes=[pltpu.VMEM((fields * width, ny), F32), dma((2,))],
        compiler_params=pltpu.CompilerParams(vmem_limit_bytes=4 * 2**20),
        cost_estimate=pl.CostEstimate(flops=6_000_000, bytes_accessed=1_400_000, transcendentals=0),
    )(value, emis_map)
    return out.reshape(lam_in.shape), grad.reshape(fields, width, ny)


def solution(mesh):
    return jax.shard_map(
        body,
        mesh=mesh,
        in_specs=(
            P("grp", None, "col", None),
            P("grp", None, "col", None),
            P("grp", None, None, None, "col", None),
            P("grp", None, None, None, "col", None),
            P("grp", None, "col", None),
            P("grp", None, "col", None),
            P("grp", "col", None),
            P(None, "grp", "col", None),
            P("grp", "col", None),
            P("grp", "col", None),
            P("grp"),
            P(),
        ),
        out_specs=(P("grp", None, "col", None), P("grp", "col", None)),
        check_vma=False,
    )
```

```python
import functools

import jax
import jax.numpy as jnp
from jax import lax
from jax.experimental import pallas as pl
from jax.experimental.pallas import tpu as pltpu
from jax.sharding import PartitionSpec as P

ADV = 2
ROWS = 8
LANES = 128
F32 = jnp.float32


def inverse_levels(kz):
    levels = len(kz) + 1
    diag = []
    for lev in range(levels):
        value = jnp.ones_like(kz[0])
        if lev > 0:
            value = value + kz[lev - 1]
        if lev < levels - 1:
            value = value + kz[lev]
        diag.append(value)
    cprime, recip = [], []
    for lev in range(levels):
        denom = diag[lev]
        if lev > 0:
            denom = denom + kz[lev - 1] * cprime[lev - 1]
        recip.append(1.0 / denom)
        cprime.append(-kz[lev] * recip[lev] if lev < levels - 1 else None)
    result = [[None] * levels for _ in range(levels)]
    for unit in range(levels):
        dprime = []
        for lev in range(levels):
            if lev < unit:
                dprime.append(jnp.zeros_like(kz[0]))
            elif lev == unit:
                dprime.append(recip[lev])
            else:
                dprime.append(kz[lev - 1] * dprime[lev - 1] * recip[lev])
        solved = dprime[levels - 1]
        result[levels - 1][unit] = solved
        for lev in range(levels - 2, -1, -1):
            solved = dprime[lev] - cprime[lev] * solved
            result[lev][unit] = solved
    return result


def up(x):
    return pltpu.roll(x, ROWS - 1, x.ndim - 2)


def down(x):
    return pltpu.roll(x, 1, x.ndim - 2)


def kernel(
    nblocks, bsize, slots, levels, cells, n,
    lam_h, conc_h, jd_h, jo_h, rows_h, cols_h, act_h, cour_h, kz_h, air_h, target_h,
    out_h,
    lam, conc, jd, jo, rows, cols, act, cour, kz, air, target,
    l0, left, right, contrib, solve, small, small_l, small_r,
    part, stat, stats, scol, gcol,
    relayed, in_sem, jo_sem, jd_sem, send_r, send_l, recv_l, recv_r, relay_send, relay_recv, ssem, stat_send, stat_recv,
):
    me = lax.axis_index("col")
    species = nblocks * bsize
    bl = bsize * ROWS
    step = bsize * bl

    def peer(k):
        return lax.rem(me + k, n)

    barrier = pltpu.get_barrier_semaphore()

    @pl.loop(1, n)
    def _(k):
        pl.semaphore_signal(
            barrier, inc=1, device_id={"col": peer(k)}, device_id_type=pl.DeviceIdType.MESH
        )

    plain = [
        pltpu.make_async_copy(src, dst, in_sem.at[k])
        for k, (src, dst) in enumerate(
            [
                (lam_h, lam), (rows_h, rows), (cols_h, cols), (act_h, act), (kz_h, kz),
                (cour_h, cour), (air_h, air), (target_h, target), (conc_h, conc),
            ]
        )
    ]

    def jo_copy(p):
        at = pl.ds(pl.multiple_of(p * step, step), step)
        return pltpu.make_async_copy(jo_h.at[at], jo.at[at], jo_sem.at[p])

    def jd_copy(c):
        at = pl.ds(pl.multiple_of(c * step, step), step)
        return pltpu.make_async_copy(jd_h.at[at], jd.at[at], jd_sem.at[c])

    for k in (0, 1, 3):
        plain[k].start()
    for p in range(slots):
        jo_copy(p).start()
    for k in (2, 4, 5, 6, 7):
        plain[k].start()
    for c in range(nblocks):
        jd_copy(c).start()
        if c == 0:
            plain[8].start()

    @pl.when(me == 0)
    def _():
        left[...] = jnp.zeros_like(left)
        small_l[...] = jnp.zeros_like(small_l)

    @pl.when(me == n - 1)
    def _():
        right[...] = jnp.zeros_like(right)
        small_r[...] = jnp.zeros_like(small_r)

    for k in (1, 3):
        plain[k].wait()

    plain[0].wait()

    @pl.loop(0, slots)
    def _(p):
        live = act[...] > p
        want = jnp.where(live, rows[pl.ds(pl.multiple_of(p * ROWS, ROWS), ROWS), :], -1)
        chosen = jnp.zeros((bsize, ROWS, LANES), F32)
        for b in range(nblocks):
            block = lam[b * bl : (b + 1) * bl, :].reshape(bsize, ROWS, LANES)
            chosen = jnp.where((want == b)[None], block, chosen)
        jo_copy(p).wait()
        acc = jnp.zeros((bsize, ROWS, LANES), F32)
        for i in range(bsize):
            at = pl.ds(pl.multiple_of(p * step + i * bl, bl), bl)
            acc = acc + jo[at, :].astype(F32).reshape(bsize, ROWS, LANES) * chosen[i][None]
        contrib[p] = acc

    for k in (2, 4, 5, 6, 7):
        plain[k].wait()

    kzs = [kz[lev] for lev in range(levels - 1)]
    inverse = inverse_levels(kzs)
    for shift in range(levels):
        for lev in range(levels):
            solve[shift, 2 * lev : 2 * lev + 2, :] = inverse[lev][(lev - shift) % levels]

    def solve_levels(x):
        total = x * solve[0]
        for shift in range(1, levels):
            total = total + pltpu.roll(x, 2 * shift, x.ndim - 2) * solve[shift]
        return total

    small[0:8, :] = cour[0:8, :]
    small[8:16, :] = cour[8:16, :]
    small[16:24, :] = solve_levels(air[...])

    pl.semaphore_wait(barrier, n - 1)

    def to_right(src, dst, ssem_, rsem):
        return pltpu.make_async_remote_copy(
            src_ref=src, dst_ref=dst, send_sem=ssem_, recv_sem=rsem,
            device_id={"col": jnp.minimum(me + 1, n - 1)}, device_id_type=pl.DeviceIdType.MESH,
        )

    def to_left(src, dst, ssem_, rsem):
        return pltpu.make_async_remote_copy(
            src_ref=src, dst_ref=dst, send_sem=ssem_, recv_sem=rsem,
            device_id={"col": jnp.maximum(me - 1, 0)}, device_id_type=pl.DeviceIdType.MESH,
        )

    def block_at(c):
        return pl.ds(pl.multiple_of(c * bl, bl), bl)

    def block_right(c):
        return to_right(l0.at[block_at(c)], left.at[block_at(c)], send_r.at[c], recv_l.at[c])

    def block_left(c):
        return to_left(l0.at[block_at(c)], right.at[block_at(c)], send_l.at[c], recv_r.at[c])

    early = nblocks // 2 - 2

    relaying = n == 16
    place4, plane = lax.rem(me, 4), me // 4
    relay_until = nblocks - 4
    from_left_flow = (place4 == 0) & (plane > 0)
    from_right_flow = (place4 == 3) & (plane < 3)
    relay_left = (place4 == 2) & (plane > 0)
    relay_right = (place4 == 1) & (plane < 3)
    share = jnp.where(place4 % 2 == 0, 2 * plane, 6 - 2 * plane)

    def takes_relay(c):
        return (c < relay_until) & (lax.rem(c * share, relay_until) < share)

    def to_relay(c, offset, sems):
        return pltpu.make_async_remote_copy(
            src_ref=l0.at[block_at(c)], dst_ref=relayed.at[block_at(c)],
            send_sem=sems.at[c], recv_sem=relay_recv.at[c],
            device_id={"col": lax.rem(me + n + offset, n)}, device_id_type=pl.DeviceIdType.MESH,
        )

    def onward(c, offset, dst, sems):
        return pltpu.make_async_remote_copy(
            src_ref=relayed.at[block_at(c)], dst_ref=dst.at[block_at(c)],
            send_sem=relay_send.at[c], recv_sem=sems.at[c],
            device_id={"col": lax.rem(me + n + offset, n)}, device_id_type=pl.DeviceIdType.MESH,
        )

    def forward(c):
        @pl.when(relay_left & takes_relay(c))
        def _():
            to_relay(c, 2, send_l).wait_recv()
            onward(c, -3, right, recv_r).start()

        @pl.when(relay_right & takes_relay(c))
        def _():
            to_relay(c, -2, send_r).wait_recv()
            onward(c, 3, left, recv_l).start()

    def send_block(c):
        if relaying:
            detour_right = from_right_flow & takes_relay(c)
            detour_left = from_left_flow & takes_relay(c)

            @pl.when(detour_right)
            def _():
                to_relay(c, -2, send_r).start()

            @pl.when(detour_left)
            def _():
                to_relay(c, 2, send_l).start()

            direct_right = (me < n - 1) & jnp.logical_not(detour_right)
            direct_left = (me > 0) & jnp.logical_not(detour_left)
        else:
            direct_right, direct_left = me < n - 1, me > 0

        @pl.when(direct_right)
        def _():
            block_right(c).start()

        @pl.when(direct_left)
        def _():
            block_left(c).start()

    small_right = to_right(small, small_l, ssem.at[0], ssem.at[1])
    small_left = to_left(small, small_r, ssem.at[2], ssem.at[3])

    @pl.when(me < n - 1)
    def _():
        small_right.start()

    @pl.when(me > 0)
    def _():
        small_left.start()

    plain[8].wait()

    @pl.loop(0, nblocks)
    def _(c):
        block = lam[block_at(c), :].reshape(bsize, ROWS, LANES)
        jd_copy(c).wait()
        acc = block
        for i in range(bsize):
            at = pl.ds(pl.multiple_of(c * step + i * bl, bl), bl)
            acc = acc + jd[at, :].astype(F32).reshape(bsize, ROWS, LANES) * block[i][None]
        for p in range(slots):
            place = cols[p * ROWS : (p + 1) * ROWS, :] == c
            acc = acc + jnp.where(place[None], contrib[p], 0.0)
        l0[block_at(c), :] = solve_levels(acc).reshape(bl, LANES)

        @pl.when(c < early)
        def _():
            send_block(c)

        amount = conc[block_at(c), :].reshape(bsize, ROWS, LANES)
        at = pl.ds(pl.multiple_of(c * bsize, bsize), bsize)
        part[0, at, :] = jnp.sum(amount * air[...][None], axis=1)
        part[1, at, :] = jnp.sum(amount * acc, axis=1)

    tail = species - LANES
    for which in range(2):
        for half, first in enumerate((0, tail)):
            square = part[which, first : first + LANES, :]
            stat[2 * which + half : 2 * which + half + 1, :] = jnp.sum(
                square.T, axis=0, keepdims=True
            )

    def stat_copy(k):
        return pltpu.make_async_remote_copy(
            src_ref=stat, dst_ref=stats.at[me], send_sem=stat_send.at[k], recv_sem=stat_recv.at[me],
            device_id={"col": peer(k)}, device_id_type=pl.DeviceIdType.MESH,
        )

    def stat_from(k):
        source = lax.rem(me + n - k, n)
        return source, pltpu.make_async_remote_copy(
            src_ref=stat, dst_ref=stats.at[source], send_sem=stat_send.at[k],
            recv_sem=stat_recv.at[source],
            device_id={"col": peer(k)}, device_id_type=pl.DeviceIdType.MESH,
        )

    @pl.loop(1, n)
    def _(k):
        stat_copy(k).start()

    @pl.loop(early, nblocks)
    def _(c):
        send_block(c)

    if relaying:

        @pl.loop(0, early)
        def _(c):
            forward(c)

    @pl.when(me > 0)
    def _():
        to_right(small, small_l, ssem.at[0], ssem.at[1]).wait_recv()

    @pl.when(me < n - 1)
    def _():
        to_left(small, small_r, ssem.at[2], ssem.at[3]).wait_recv()

    even = lax.rem(lax.broadcasted_iota(jnp.int32, (ROWS, LANES), 0), 2) == 0

    def swap(x):
        return jnp.where(even, up(x), down(x))

    a, b = small[0:8, :], small[8:16, :]
    c = 1.0 - a - b
    al, bl_ = small_l[0:8, :], small_l[8:16, :]
    cl = 1.0 - al - bl_
    ar, br = small_r[0:8, :], small_r[8:16, :]
    cr = 1.0 - ar - br
    own_same = c * c + jnp.where(even, b * swap(al) + a * swap(b), b * swap(a) + a * swap(br))
    own_swap = jnp.where(even, a, b) * (c + swap(c))
    left_same = b * jnp.where(even, swap(bl_), swap(b))
    left_up = jnp.where(even, b * (c + swap(cl)), 0.0)
    right_same = a * jnp.where(even, swap(a), swap(ar))
    right_down = jnp.where(even, 0.0, a * (c + swap(cr)))

    def advect(mid, lt, rt):
        return (
            own_same * mid
            + own_swap * jnp.where(even, up(mid), down(mid))
            + left_same * lt
            + left_up * up(lt)
            + right_same * rt
            + right_down * down(rt)
        )

    air_out = advect(small[16:24, :], small_l[16:24, :], small_r[16:24, :])

    def add_stat(k, total):
        source, copy = stat_from(k)
        copy.wait_recv()
        return total + stats[source]

    total = lax.fori_loop(1, n, add_stat, stat[...])
    for half, first in enumerate((0, tail)):
        mass = total[half : half + 1, :]
        quad = total[2 + half : 3 + half, :]
        scale = target[:, first : first + LANES] * float(cells) / mass
        gain = scale * quad / mass
        scol[first : first + LANES, :] = jnp.broadcast_to(scale, (LANES, LANES)).T
        gcol[first : first + LANES, :] = jnp.broadcast_to(gain, (LANES, LANES)).T

    @pl.loop(0, nblocks)
    def _(c):
        if relaying:

            @pl.when(c < relay_until - early)
            def _():
                forward(c + early)

        @pl.when(me > 0)
        def _():
            block_right(c).wait_recv()

        @pl.when(me < n - 1)
        def _():
            block_left(c).wait_recv()

        at = block_at(c)
        shape = (bsize, ROWS, LANES)
        moved = advect(l0[at, :].reshape(shape), left[at, :].reshape(shape), right[at, :].reshape(shape))
        names = pl.ds(pl.multiple_of(c * bsize, bsize), bsize)
        result = scol[names, :][:, None, :] * moved - gcol[names, :][:, None, :] * air_out[None]
        out_h[at, :] = result.reshape(bl, LANES)

    @pl.loop(0, nblocks)
    def _(c):
        @pl.when(me < n - 1)
        def _():
            block_right(c).wait_send()

        @pl.when(me > 0)
        def _():
            block_left(c).wait_send()

        if relaying:

            @pl.when((relay_left | relay_right) & takes_relay(c))
            def _():
                onward(c, 3, left, recv_l).wait_send()

    @pl.when(me < n - 1)
    def _():
        to_right(small, small_l, ssem.at[0], ssem.at[1]).wait_send()

    @pl.when(me > 0)
    def _():
        to_left(small, small_r, ssem.at[2], ssem.at[3]).wait_send()

    @pl.loop(1, n)
    def _(k):
        stat_copy(k).wait_send()


def finish(nblocks, value, emis, out_h, grad_h, grad, sem):
    species, fields = emis.shape[1], emis.shape[0]
    lam_copy = pltpu.make_async_copy(value, out_h, sem.at[0])
    lam_copy.start()
    for x in range(2):
        ground = value[pl.ds(x, species, stride=ROWS), :]
        grad[pl.ds(x, fields, stride=2), :] = jnp.dot(
            emis[...], ground, precision=lax.Precision.HIGHEST, preferred_element_type=F32
        )
    grad_copy = pltpu.make_async_copy(grad, grad_h, sem.at[1])
    grad_copy.start()
    lam_copy.wait()
    grad_copy.wait()


def body(
    lam_in, conc, jac_diag, jac_off, block_rows, block_cols, active, courant, kz, airmass, target, emis_map
):
    species, levels, width, ny = lam_in.shape
    n = lax.axis_size("col")
    nblocks, bsize = jac_diag.shape[:2]
    slots = jac_off.shape[0]
    cells = levels * width * ny * n
    fields = emis_map.shape[0]

    def flat(x):
        return x.reshape(-1, ny)

    operands = [
        flat(lam_in), flat(conc), flat(jac_diag), flat(jac_off), flat(block_rows), flat(block_cols),
        flat(active), flat(courant), kz, flat(airmass), target.reshape(1, species),
    ]
    big = (species * ROWS, ny)
    held = [pltpu.VMEM(x.shape, x.dtype) for x in operands]
    dma = pltpu.SemaphoreType.DMA
    whole = pl.BlockSpec(memory_space=pltpu.VMEM)
    value = pl.pallas_call(
        functools.partial(kernel, nblocks, bsize, slots, levels, cells, n),
        out_shape=pltpu.VMEM(big, F32),
        in_specs=[pl.BlockSpec(memory_space=pltpu.HBM)] * len(operands),
        out_specs=whole,
        scratch_shapes=held
        + [
            pltpu.VMEM(big, F32), pltpu.VMEM(big, F32), pltpu.VMEM(big, F32),
            pltpu.VMEM((slots, bsize, ROWS, ny), F32),
            pltpu.VMEM((levels, ROWS, ny), F32),
            pltpu.VMEM((24, ny), F32), pltpu.VMEM((24, ny), F32), pltpu.VMEM((24, ny), F32),
            pltpu.VMEM((2, species, ny), F32),
            pltpu.VMEM((4, ny), F32), pltpu.VMEM((n, 4, ny), F32),
            pltpu.VMEM((species, ny), F32), pltpu.VMEM((species, ny), F32),
            pltpu.VMEM(big, F32),
            dma((9,)), dma((slots,)), dma((nblocks,)),
            dma((nblocks,)), dma((nblocks,)), dma((nblocks,)), dma((nblocks,)),
            dma((nblocks,)), dma((nblocks,)), dma((4,)), dma((n,)), dma((n,)),
        ],
        compiler_params=pltpu.CompilerParams(
            collective_id=0, has_side_effects=True, vmem_limit_bytes=60 * 2**20
        ),
        cost_estimate=pl.CostEstimate(flops=8_000_000, bytes_accessed=10_000_000, transcendentals=0),
    )(*operands)
    hbm = pl.BlockSpec(memory_space=pltpu.HBM)
    out, grad = pl.pallas_call(
        functools.partial(finish, nblocks),
        out_shape=(
            jax.ShapeDtypeStruct(big, F32),
            jax.ShapeDtypeStruct((fields * width, ny), F32),
        ),
        in_specs=[whole, whole],
        out_specs=(hbm, hbm),
        scratch_shapes=[pltpu.VMEM((fields * width, ny), F32), dma((2,))],
        compiler_params=pltpu.CompilerParams(vmem_limit_bytes=4 * 2**20),
        cost_estimate=pl.CostEstimate(flops=6_000_000, bytes_accessed=1_400_000, transcendentals=0),
    )(value, emis_map)
    return out.reshape(lam_in.shape), grad.reshape(fields, width, ny)


def solution(mesh):
    return jax.shard_map(
        body,
        mesh=mesh,
        in_specs=(
            P("grp", None, "col", None),
            P("grp", None, "col", None),
            P("grp", None, None, None, "col", None),
            P("grp", None, None, None, "col", None),
            P("grp", None, "col", None),
            P("grp", None, "col", None),
            P("grp", "col", None),
            P(None, "grp", "col", None),
            P("grp", "col", None),
            P("grp", "col", None),
            P("grp"),
            P(),
        ),
        out_specs=(P("grp", None, "col", None), P("grp", "col", None)),
        check_vma=False,
    )
```
